128 devices in a mesh: lat: 16 (over y, x), lev: 8 (over z, core).
Axes of the slice: x: 4, y: 4, z: 4, core: 2. Of those that a mesh axis runs over, the one named last changes fastest.
Arguments:
- fourier: bfloat16 [32, 2, 2560, 1280], P('lev', None, 'lat'), may hold values from -6 to 6
- loop_len: int32 [1280], replicated, may hold values from 20 to 5148, as said below
- pair_m: int32 [640], replicated, may hold values from 0 to 639, each once
- legendre: bfloat16 [640, 1281, 1280], P(('lat', 'lev')), may hold values from -0.15625 to 0.15625
Outputs:
- spectrum: float32 [640, 1281, 64], P(('lat', 'lev'))
The draws below stay inside these ranges and needn't reach their ends.
Inputs may be any that keep to these rules, and one draw needn't show every extreme that they name: `loop_len`: loop lengths of one hemisphere from the pole to the equator, each a multiple of 4; the loop next to the pole has the fewest points, the one next to the equator the most. Slot s holds the wavenumbers pair_m[s] and 1279 - pair_m[s]; every value appears once.
All inputs are finite; a program needn't handle non-finite values.
Results may differ from the reference program's by a relative error of at most 0.0031.
Values may be sent and summed in bfloat16 or wider, within the bound.
No kernel may reach another device: no remote copies, remote signals or barrier semaphores. Data moves between devices by JAX's collectives and lax.ppermute only.
A program may use at most 128 MiB of HBM per device.

```python
import jax
import jax.numpy as jnp
from jax import lax

HEMISPHERE_LATS = 1280
MW = 1280
LEVELS = 32
NLAT = 2560
WAVENUMBER_PAIRS = 640
PAIR_SLOTS = 1281
NSYM = 641


def draw_loop_len(key, part):
    key = jax.random.fold_in(key, 11)
    steps = jax.random.randint(key, (HEMISPHERE_LATS,), 0, 4)
    steps = steps.at[0].set(0).at[HEMISPHERE_LATS - 1].set(3)
    return (20 + 4 * jnp.arange(HEMISPHERE_LATS, dtype=jnp.int32) + 4 * steps).astype(jnp.int32)


def shard_levels(own_key, dims, split, low, top_value):
    factor_of = 1.0
    for dim, shards_of in split:
        heights = jax.random.uniform(jax.random.fold_in(jax.random.fold_in(own_key, 6), dim), (shards_of,), jnp.float32, low / len(split), top_value / len(split))
        factor_of = factor_of * jnp.repeat(jnp.exp(heights), dims[dim] // shards_of).reshape((-1,) + (1,) * (len(dims) - 1 - dim))
    return factor_of


def scatter_about(rng, shape, scale, limit, cuts=(), kind=jnp.bfloat16):
    drawn = scale * jax.random.normal(rng, shape, jnp.float32)
    if cuts:
        drawn = drawn * shard_levels(rng, shape, cuts, -0.22, 0.18)
    return jnp.clip(drawn, -limit, limit).astype(kind)


def setup_inputs(seed: int = 0) -> dict:
    key_of = jax.random.split(jax.random.key(seed), 5)
    fourier = scatter_about(key_of[0], (LEVELS, 2, NLAT, MW), 1.0, 6.0, ((0, 8), (2, 16)))
    loop_len = draw_loop_len(jax.random.fold_in(key_of[4], 71), 0)
    pair_m = jax.random.permutation(key_of[2], WAVENUMBER_PAIRS).astype(jnp.int32)
    legendre = scatter_about(key_of[3], (WAVENUMBER_PAIRS, PAIR_SLOTS, HEMISPHERE_LATS), HEMISPHERE_LATS ** -0.5, 0.15625, ((0, 128),))
    return dict(fourier=fourier, loop_len=loop_len, pair_m=pair_m, legendre=legendre)


def reference(fourier, loop_len, pair_m, legendre):
    limits = jnp.minimum(MW, loop_len // 2)
    inside = jnp.arange(MW, dtype=jnp.int32)[None, :] < limits[:, None]
    north = jnp.where(inside, fourier[:, :, :HEMISPHERE_LATS, :], jnp.zeros((), fourier.dtype)).astype(jnp.float32)
    south = jnp.where(inside, fourier[:, :, HEMISPHERE_LATS:, :], jnp.zeros((), fourier.dtype)).astype(jnp.float32)
    symmetric = (north + south).astype(jnp.bfloat16)
    antisymmetric = (north - south).astype(jnp.bfloat16)
    sym_waves = symmetric.transpose(3, 2, 1, 0).reshape(MW, HEMISPHERE_LATS, 2 * LEVELS)
    anti_waves = antisymmetric.transpose(3, 2, 1, 0).reshape(MW, HEMISPHERE_LATS, 2 * LEVELS)
    sym_index = jnp.arange(NSYM, dtype=jnp.int32)
    anti_index = jnp.arange(MW // 2, dtype=jnp.int32)

    def each_pair_slots(inputs):
        table_rows, lower = inputs
        upper = MW - 1 - lower
        table_float = table_rows.astype(jnp.float32)
        sym_low = lax.dynamic_index_in_dim(sym_waves, lower, 0, keepdims=False).astype(jnp.float32)
        sym_high = lax.dynamic_index_in_dim(sym_waves, upper, 0, keepdims=False).astype(jnp.float32)
        antisym_lower = lax.dynamic_index_in_dim(anti_waves, lower, 0, keepdims=False).astype(jnp.float32)
        anti_high = lax.dynamic_index_in_dim(anti_waves, upper, 0, keepdims=False).astype(jnp.float32)
        sym_table = table_float[:NSYM]
        anti_table = table_float[NSYM:]
        sym_part = jnp.where((sym_index < (MW - lower + 1) // 2)[:, None],
                             jnp.dot(sym_table, sym_low, precision=lax.Precision.HIGHEST),
                             jnp.dot(sym_table, sym_high, precision=lax.Precision.HIGHEST))
        anti_part = jnp.where((anti_index < (MW - lower) // 2)[:, None],
                              jnp.dot(anti_table, antisym_lower, precision=lax.Precision.HIGHEST),
                              jnp.dot(anti_table, anti_high, precision=lax.Precision.HIGHEST))
        return jnp.concatenate([sym_part, anti_part], 0)

    return lax.map(each_pair_slots, (legendre, pair_m))
```

```python
import functools

import jax
import jax.numpy as jnp
from jax import lax
from jax.experimental import pallas as pl
from jax.experimental.pallas import tpu as pltpu
from jax.sharding import PartitionSpec as P

LANES = 128
SLAB = 32
CHUNK = 104
NT = (((1,), (1,)), ((), ()))


def pick_kernel(pair_ref, len_ref, four_ref, out_ref, table, main, tail, wide):
    parts, band, waves = four_ref.shape
    half = waves // 2
    owners, slots = pair_ref.shape
    bands = len_ref.shape[0]
    place = lax.rem(lax.axis_index("lat"), bands)
    turn = lax.rem(place, 4)

    lane = lax.broadcasted_iota(jnp.int32, (owners, half), 1)
    for s in range(slots):
        low = pair_ref[:, s : s + 1]
        rows = pl.ds(s * owners, owners)
        table[0, rows, :] = jnp.where(lane == low, 1.0, 0.0).astype(jnp.bfloat16)
        table[1, rows, :] = jnp.where(lane == half - 1 - low, 1.0, 0.0).astype(jnp.bfloat16)

    limit = jnp.minimum(waves, lax.shift_right_logical(len_ref[pl.ds(place, 1), :], 1))
    column = jnp.transpose(jnp.broadcast_to(limit, (LANES, limit.shape[1])))
    lane = lax.broadcasted_iota(jnp.int32, (SLAB, LANES), 1)
    for slab in range(band // SLAB):
        edge = column[slab * SLAB : (slab + 1) * SLAB]
        for tile in range(waves // LANES):
            keep = jnp.where(lane + tile * LANES < edge, 1.0, 0.0).astype(jnp.bfloat16)
            cols = pl.ds(tile * LANES, LANES)
            for t in range(parts):
                value = four_ref[t, pl.ds(slab * SLAB, SLAB), cols] * keep
                if slab < 4:
                    start = t * LANES + lax.rem(slab + turn, 4) * SLAB
                    main[pl.ds(pl.multiple_of(start, SLAB), SLAB), cols] = value
                else:
                    tail[pl.ds(t * SLAB, SLAB), cols] = value

    def picked(k, rows):
        return lax.dot_general(
            table[k], rows[:, half * k : half * (k + 1)], NT, preferred_element_type=jnp.float32
        )

    for n in range(parts // 2):
        rows = main[pl.ds(2 * LANES * n, 2 * LANES), :]
        for k in range(2):
            value = picked(k, rows)
            for s in range(slots):
                for h in range(2):
                    start = 16 * s + 8 * k + 2 * n + h
                    wide[pl.ds(start, owners, stride=CHUNK), :] = value[
                        s * owners : (s + 1) * owners, h * LANES : (h + 1) * LANES
                    ]

    lane = lax.broadcasted_iota(jnp.int32, (owners, LANES), 1)
    rows = tail[...]
    values = [picked(k, rows) for k in range(2)]

    def turned(k, s, h, by):
        value = values[k][s * owners : (s + 1) * owners, h * LANES : (h + 1) * LANES]
        by = (by * SLAB) % LANES
        return pltpu.roll(value, by, 1) if by else value

    for h in range(2):
        for part in range(4):
            for k in range(2):
                out = turned(k, 3, h, 3 - part)
                for s in (2, 1, 0):
                    out = jnp.where(lane < SLAB * (s + 1), turned(k, s, h, s - part), out)
                start = 16 * slots + 8 * k + 4 * h + part
                wide[pl.ds(start, owners, stride=CHUNK), :] = out
            out = jnp.where(lane < SLAB, turned(0, 4, h, -part), turned(1, 4, h, 1 - part))
            start = 16 * slots + 16 + 4 * h + part
            wide[pl.ds(start, owners, stride=CHUNK), :] = out

    block = 16 * CHUNK

    def pack(i, carry):
        rows = pl.ds(pl.multiple_of(i * block, block), block)
        out_ref[rows, :] = wide[rows, :].astype(jnp.bfloat16)
        return carry

    lax.fori_loop(0, owners * CHUNK // block, pack, 0)


def sum_kernel(pair_ref, got_ref, leg_ref, out_ref, leg, both, rows64, out, leg_sem, out_sem):
    slots, count, loops = leg_ref.shape
    waves = 2 * pair_ref.shape[0]
    half = waves // 2
    groups = loops // (5 * LANES)
    peers = got_ref.shape[0] // CHUNK
    levs = peers // (8 * groups)
    south = peers // 2 * CHUNK
    owner = lax.axis_index("lat") * lax.axis_size("lev") + lax.axis_index("lev")

    fetches = [pltpu.make_async_copy(leg_ref.at[s], leg.at[s], leg_sem.at[s]) for s in range(slots)]
    for fetch in fetches:
        fetch.start()

    lane = lax.broadcasted_iota(jnp.int32, (16, LANES), 1)
    signs = (1.0, -1.0)

    def pair_of(src, start, size):
        rows = pl.ds(src * CHUNK + start, size)
        north = got_ref[rows, :].astype(jnp.float32)
        rows = pl.ds(src * CHUNK + south + start, size)
        return north, got_ref[rows, :].astype(jnp.float32)

    def combined(pair):
        return pair[0] + pair[1], pair[0] - pair[1]

    def turned(value, by):
        by = (by * SLAB) % LANES
        return pltpu.roll(value, by, 1) if by else value

    for s in range(slots):
        for j in range(levs):
            for g in range(groups):
                mains, tails = [], []
                for b in range(4):
                    src = (4 * g + b) * levs + j
                    mains.append(combined(pair_of(src, 16 * s, 16)))
                    if s < 4:
                        ends = combined(pair_of(src, 16 * slots, 16))
                        tails.append([turned(e, b - s) for e in ends])
                    else:
                        ends = combined(pair_of(src, 16 * slots + 16, 8))
                        tails.append([jnp.concatenate([turned(e, b), turned(e, b - 1)], 0) for e in ends])
                for p in range(2):
                    m = [x[p] for x in mains]
                    e = [x[p] for x in tails]
                    tiles = (
                        m[0],
                        jnp.where(lane < 32, e[0], m[1]),
                        jnp.where(lane < 32, m[1], jnp.where(lane < 64, e[1], m[2])),
                        jnp.where(lane < 64, m[2], jnp.where(lane < 96, e[2], m[3])),
                        jnp.where(lane < 96, m[3], e[3]),
                    )
                    for i, tile in enumerate(tiles):
                        cols = pl.ds((5 * g + i) * LANES, LANES)
                        both[p, pl.ds(16 * j, 16), cols] = tile.astype(jnp.bfloat16)

        fetches[s].wait()
        dot = functools.partial(lax.dot_general, dimension_numbers=NT, preferred_element_type=jnp.float32)
        sym = dot(both[0], leg[s, pl.ds(0, half), :])
        anti = dot(both[1], leg[s, pl.ds(half, count - half), :])
        middle = dot(both[0], leg[s, pl.ds(half, 16), :])

        low = pair_ref[owner * slots + s]
        sym_limit = lax.shift_right_logical(waves - low + 1, 1)
        anti_limit = lax.shift_right_logical(waves - low, 1) + half + 1
        for j in range(levs):
            a, b = pl.ds(16 * j, 8), pl.ds(16 * j + 8, 8)
            first = slice(16 * j, 16 * j + 8)
            second = slice(16 * j + 8, 16 * j + 16)
            tiles = half // LANES
            for i in range(tiles):
                at = lax.broadcasted_iota(jnp.int32, (8, LANES), 1) + i * LANES
                cols = slice(i * LANES, (i + 1) * LANES)
                rows64[i, pl.ds(8 * j, 8), :] = jnp.where(at < sym_limit, sym[first, cols], sym[second, cols])
            for i in range(tiles + 1):
                width = min(LANES, count - half - i * LANES)
                at = lax.broadcasted_iota(jnp.int32, (8, width), 1) + half + i * LANES
                cols = slice(i * LANES, i * LANES + width)
                value = jnp.where(at < anti_limit, anti[first, cols], anti[second, cols])
                if i == 0:
                    mid = jnp.where(half < sym_limit, middle[first, :1], middle[second, :1])
                    value = jnp.where(at == half, mid, value)
                rows64[tiles + i, pl.ds(8 * j, 8), :width] = value
        for i in range(rows64.shape[0]):
            width = min(LANES, count - i * LANES)
            for c in range(2):
                for v in range(levs // 2):
                    value = rows64[i, pl.ds(16 * v + c, 8, stride=2), :]
                    out[s, pl.ds(4 * levs * c + 8 * v, 8), pl.ds(i * LANES, width)] = value[:, :width]
        pltpu.make_async_copy(out.at[s], out_ref.at[s], out_sem.at[s]).start()
    for s in range(slots):
        pltpu.make_async_copy(out.at[s], out_ref.at[s], out_sem.at[s]).wait()


def shards(fourier, loop_len, pair_m, legendre):
    levels, parts, band, waves = fourier.shape
    slots, count, loops = legendre.shape
    owners = pair_m.shape[0] // slots
    half = waves // 2
    bands = loops // band
    vmem = pl.BlockSpec(memory_space=pltpu.VMEM)
    lengths = jnp.pad(loop_len.reshape(bands, band), ((0, 0), (0, 2 * LANES - band)))
    outgoing = pl.pallas_call(
        pick_kernel,
        out_shape=jax.ShapeDtypeStruct((owners * CHUNK, LANES), jnp.bfloat16),
        in_specs=[vmem] * 3,
        out_specs=vmem,
        scratch_shapes=[
            pltpu.VMEM((2, owners * slots, half), jnp.bfloat16),
            pltpu.VMEM((levels * parts * LANES, waves), jnp.bfloat16),
            pltpu.VMEM((levels * parts * SLAB, waves), jnp.bfloat16),
            pltpu.VMEM((owners * CHUNK, LANES), jnp.float32),
        ],
        compiler_params=pltpu.CompilerParams(vmem_limit_bytes=50 * 2**20),
        name="pick",
    )(pair_m.reshape(owners, slots), lengths, fourier.reshape(levels * parts, band, waves))
    arrived = lax.all_to_all(
        outgoing.reshape(owners, CHUNK, LANES), ("lat", "lev"), split_axis=0, concat_axis=0, tiled=True
    )
    out = pl.pallas_call(
        sum_kernel,
        out_shape=jax.ShapeDtypeStruct((slots, 64, count), jnp.float32),
        in_specs=[
            pl.BlockSpec(memory_space=pltpu.SMEM),
            vmem,
            pl.BlockSpec(memory_space=pl.ANY),
        ],
        out_specs=pl.BlockSpec(memory_space=pl.ANY),
        scratch_shapes=[
            pltpu.VMEM((slots, count, loops), jnp.bfloat16),
            pltpu.VMEM((2, 128, loops), jnp.bfloat16),
            pltpu.VMEM((count // LANES + 1, 64, LANES), jnp.float32),
            pltpu.VMEM((slots, 64, count), jnp.float32),
            pltpu.SemaphoreType.DMA((slots,)),
            pltpu.SemaphoreType.DMA((slots,)),
        ],
        compiler_params=pltpu.CompilerParams(vmem_limit_bytes=50 * 2**20),
        name="transform",
    )(pair_m, arrived.reshape(owners * CHUNK, LANES), legendre)
    return jnp.transpose(out, (0, 2, 1))


def solution(mesh):
    return jax.shard_map(
        shards,
        mesh=mesh,
        in_specs=(P("lev", None, "lat", None), P(), P(), P(("lat", "lev"), None, None)),
        out_specs=P(("lat", "lev"), None, None),
        check_vma=False,
    )
```

```python
import functools

import jax
import jax.numpy as jnp
from jax import lax
from jax.experimental import pallas as pl
from jax.experimental.pallas import tpu as pltpu
from jax.sharding import PartitionSpec as P

LANES = 128
SLAB = 32
CHUNK = 104
NT = (((1,), (1,)), ((), ()))


def pick_kernel(
    pair_hbm, len_hbm, four_ref, leg_ref, out_ref, held_ref, pair_ref, len_ref, four, column, lows, table, main, tail, wide, sems
):
    parts, band, waves = four_ref.shape
    half = waves // 2
    slots = held_ref.shape[0]
    owners = pair_ref.shape[0] * LANES // slots
    place = lax.rem(lax.axis_index("lat"), len_ref.shape[0] * LANES // band)
    turn = lax.rem(place, 4)

    small = [
        pltpu.make_async_copy(pair_hbm, pair_ref, sems.at[parts + slots]),
        pltpu.make_async_copy(len_hbm, len_ref, sems.at[parts + slots + 1]),
    ]
    fetches = [pltpu.make_async_copy(four_ref.at[t], four.at[t], sems.at[t]) for t in range(parts)]
    fetches += [
        pltpu.make_async_copy(leg_ref.at[s], held_ref.at[s], sems.at[parts + s]) for s in range(slots)
    ]
    for fetch in small + fetches:
        fetch.start()
    for fetch in small:
        fetch.wait()

    def column_of(row):
        return jnp.transpose(jnp.broadcast_to(row, (LANES, LANES)))

    for n in range(pair_ref.shape[0]):
        lows[pl.ds(n * LANES, LANES), :] = column_of(pair_ref[pl.ds(n, 1), :])
    for s in range(slots):
        low = lows[pl.ds(s, owners, stride=slots), :]
        rows = pl.ds(s * owners, owners)
        for tile in range(half // LANES):
            lane = lax.broadcasted_iota(jnp.int32, (owners, LANES), 1) + tile * LANES
            cols = pl.ds(tile * LANES, LANES)
            table[0, rows, cols] = jnp.where(lane == low, 1.0, 0.0).astype(jnp.bfloat16)
            table[1, rows, cols] = jnp.where(lane == half - 1 - low, 1.0, 0.0).astype(jnp.bfloat16)

    first = lax.div(place * band, LANES)
    for n in range(2):
        limit = jnp.minimum(waves, lax.shift_right_logical(len_ref[pl.ds(first + n, 1), :], 1))
        column[pl.ds(n * LANES, LANES), :] = column_of(limit)
    lane = lax.broadcasted_iota(jnp.int32, (SLAB, LANES), 1)
    for t in range(parts):
        fetches[t].wait()
    for slab in range(band // SLAB):
        edge = column[pl.ds(pl.multiple_of((turn + slab) * SLAB, SLAB), SLAB), :]
        for tile in range(waves // LANES):
            keep = jnp.where(lane + tile * LANES < edge, 1.0, 0.0).astype(jnp.bfloat16)
            cols = pl.ds(tile * LANES, LANES)
            for t in range(parts):
                value = four[t, pl.ds(slab * SLAB, SLAB), cols] * keep
                if slab < 4:
                    start = t * LANES + lax.rem(slab + turn, 4) * SLAB
                    main[pl.ds(pl.multiple_of(start, SLAB), SLAB), cols] = value
                else:
                    tail[pl.ds(t * SLAB, SLAB), cols] = value

    def picked(k, rows):
        return lax.dot_general(
            table[k], rows[:, half * k : half * (k + 1)], NT, preferred_element_type=jnp.float32
        )

    for n in range(parts // 2):
        rows = main[pl.ds(2 * LANES * n, 2 * LANES), :]
        for k in range(2):
            value = picked(k, rows)
            for s in range(slots):
                for h in range(2):
                    start = 16 * s + 8 * k + 2 * n + h
                    wide[pl.ds(start, owners, stride=CHUNK), :] = value[
                        s * owners : (s + 1) * owners, h * LANES : (h + 1) * LANES
                    ]

    lane = lax.broadcasted_iota(jnp.int32, (owners, LANES), 1)
    rows = tail[...]
    values = [picked(k, rows) for k in range(2)]

    def turned(k, s, h, by):
        value = values[k][s * owners : (s + 1) * owners, h * LANES : (h + 1) * LANES]
        by = (by * SLAB) % LANES
        return pltpu.roll(value, by, 1) if by else value

    for h in range(2):
        for part in range(4):
            for k in range(2):
                out = turned(k, 3, h, 3 - part)
                for s in (2, 1, 0):
                    out = jnp.where(lane < SLAB * (s + 1), turned(k, s, h, s - part), out)
                start = 16 * slots + 8 * k + 4 * h + part
                wide[pl.ds(start, owners, stride=CHUNK), :] = out
            out = jnp.where(lane < SLAB, turned(0, 4, h, -part), turned(1, 4, h, 1 - part))
            start = 16 * slots + 16 + 4 * h + part
            wide[pl.ds(start, owners, stride=CHUNK), :] = out

    block = 16 * CHUNK

    def pack(i, carry):
        rows = pl.ds(pl.multiple_of(i * block, block), block)
        out_ref[rows, :] = wide[rows, :].astype(jnp.bfloat16)
        return carry

    lax.fori_loop(0, owners * CHUNK // block, pack, 0)
    for fetch in fetches[parts:]:
        fetch.wait()


def sum_kernel(pair_ref, got_ref, leg, out_ref, both, rows64, out, out_sem):
    slots, count, loops = leg.shape
    waves = 2 * pair_ref.shape[0]
    half = waves // 2
    groups = loops // (5 * LANES)
    peers = got_ref.shape[0] // CHUNK
    levs = peers // (8 * groups)
    south = peers // 2 * CHUNK
    owner = lax.axis_index("lat") * lax.axis_size("lev") + lax.axis_index("lev")

    lane = lax.broadcasted_iota(jnp.int32, (16, LANES), 1)

    def pair_of(src, start, size):
        rows = pl.ds(src * CHUNK + start, size)
        north = got_ref[rows, :].astype(jnp.float32)
        rows = pl.ds(src * CHUNK + south + start, size)
        return north, got_ref[rows, :].astype(jnp.float32)

    def combined(pair):
        return pair[0] + pair[1], pair[0] - pair[1]

    def turned(value, by):
        by = (by * SLAB) % LANES
        return pltpu.roll(value, by, 1) if by else value

    for s in range(slots):
        for j in range(levs):
            for g in range(groups):
                mains, tails = [], []
                for b in range(4):
                    src = (4 * g + b) * levs + j
                    mains.append(combined(pair_of(src, 16 * s, 16)))
                    if s < 4:
                        ends = combined(pair_of(src, 16 * slots, 16))
                        tails.append([turned(e, b - s) for e in ends])
                    else:
                        ends = combined(pair_of(src, 16 * slots + 16, 8))
                        tails.append([jnp.concatenate([turned(e, b), turned(e, b - 1)], 0) for e in ends])
                for p in range(2):
                    m = [x[p] for x in mains]
                    e = [x[p] for x in tails]
                    tiles = (
                        m[0],
                        jnp.where(lane < 32, e[0], m[1]),
                        jnp.where(lane < 32, m[1], jnp.where(lane < 64, e[1], m[2])),
                        jnp.where(lane < 64, m[2], jnp.where(lane < 96, e[2], m[3])),
                        jnp.where(lane < 96, m[3], e[3]),
                    )
                    for i, tile in enumerate(tiles):
                        cols = pl.ds((5 * g + i) * LANES, LANES)
                        both[p, pl.ds(16 * j, 16), cols] = tile.astype(jnp.bfloat16)

        dot = functools.partial(lax.dot_general, dimension_numbers=NT, preferred_element_type=jnp.float32)
        sym = dot(both[0], leg[s, pl.ds(0, half), :])
        anti = dot(both[1], leg[s, pl.ds(half, count - half), :])
        middle = dot(both[0], leg[s, pl.ds(half, 16), :])

        low = pair_ref[owner * slots + s]
        sym_limit = lax.shift_right_logical(waves - low + 1, 1)
        anti_limit = lax.shift_right_logical(waves - low, 1) + half + 1
        for j in range(levs):
            first = slice(16 * j, 16 * j + 8)
            second = slice(16 * j + 8, 16 * j + 16)
            tiles = half // LANES
            for i in range(tiles):
                at = lax.broadcasted_iota(jnp.int32, (8, LANES), 1) + i * LANES
                cols = slice(i * LANES, (i + 1) * LANES)
                rows64[i, pl.ds(8 * j, 8), :] = jnp.where(at < sym_limit, sym[first, cols], sym[second, cols])
            for i in range(tiles + 1):
                width = min(LANES, count - half - i * LANES)
                at = lax.broadcasted_iota(jnp.int32, (8, width), 1) + half + i * LANES
                cols = slice(i * LANES, i * LANES + width)
                value = jnp.where(at < anti_limit, anti[first, cols], anti[second, cols])
                if i == 0:
                    mid = jnp.where(half < sym_limit, middle[first, :1], middle[second, :1])
                    value = jnp.where(at == half, mid, value)
                rows64[tiles + i, pl.ds(8 * j, 8), :width] = value
        for i in range(rows64.shape[0]):
            width = min(LANES, count - i * LANES)
            for c in range(2):
                for v in range(levs // 2):
                    value = rows64[i, pl.ds(16 * v + c, 8, stride=2), :]
                    out[s, pl.ds(4 * levs * c + 8 * v, 8), pl.ds(i * LANES, width)] = value[:, :width]
        pltpu.make_async_copy(out.at[s], out_ref.at[s], out_sem.at[s]).start()
    for s in range(slots):
        pltpu.make_async_copy(out.at[s], out_ref.at[s], out_sem.at[s]).wait()


def in_hbm(value):
    return pltpu.with_memory_space_constraint(value, pltpu.HBM)


def shards(fourier, loop_len, pair_m, legendre):
    levels, parts, band, waves = fourier.shape
    slots, count, loops = legendre.shape
    owners = pair_m.shape[0] // slots
    half = waves // 2
    vmem = pl.BlockSpec(memory_space=pltpu.VMEM)
    hbm = pl.BlockSpec(memory_space=pltpu.HBM)
    outgoing, held = pl.pallas_call(
        pick_kernel,
        out_shape=(
            jax.ShapeDtypeStruct((owners * CHUNK, LANES), jnp.bfloat16),
            pltpu.VMEM(legendre.shape, legendre.dtype),
        ),
        in_specs=[hbm] * 4,
        out_specs=(vmem, vmem),
        scratch_shapes=[
            pltpu.VMEM((owners * slots // LANES, LANES), jnp.int32),
            pltpu.VMEM((loops // LANES, LANES), jnp.int32),
            pltpu.VMEM((levels * parts, band, waves), jnp.bfloat16),
            pltpu.VMEM((2 * LANES, LANES), jnp.int32),
            pltpu.VMEM((owners * slots, LANES), jnp.int32),
            pltpu.VMEM((2, owners * slots, half), jnp.bfloat16),
            pltpu.VMEM((levels * parts * LANES, waves), jnp.bfloat16),
            pltpu.VMEM((levels * parts * SLAB, waves), jnp.bfloat16),
            pltpu.VMEM((owners * CHUNK, LANES), jnp.float32),
            pltpu.SemaphoreType.DMA((levels * parts + slots + 2,)),
        ],
        compiler_params=pltpu.CompilerParams(vmem_limit_bytes=32 * 2**20),
        name="pick",
    )(
        in_hbm(pair_m.reshape(-1, LANES)),
        in_hbm(loop_len.reshape(-1, LANES)),
        in_hbm(fourier.reshape(levels * parts, band, waves)),
        in_hbm(legendre),
    )
    arrived = lax.all_to_all(
        outgoing.reshape(owners, CHUNK, LANES), ("lat", "lev"), split_axis=0, concat_axis=0, tiled=True
    )
    out = pl.pallas_call(
        sum_kernel,
        out_shape=jax.ShapeDtypeStruct((slots, 64, count), jnp.float32),
        in_specs=[
            pl.BlockSpec(memory_space=pltpu.SMEM),
            vmem,
            vmem,
        ],
        out_specs=pl.BlockSpec(memory_space=pl.ANY),
        scratch_shapes=[
            pltpu.VMEM((2, 128, loops), jnp.bfloat16),
            pltpu.VMEM((count // LANES + 1, 64, LANES), jnp.float32),
            pltpu.VMEM((slots, 64, count), jnp.float32),
            pltpu.SemaphoreType.DMA((slots,)),
        ],
        compiler_params=pltpu.CompilerParams(vmem_limit_bytes=16 * 2**20),
        name="transform",
    )(pair_m, arrived.reshape(owners * CHUNK, LANES), held)
    return jnp.transpose(out, (0, 2, 1))


def solution(mesh):
    return jax.shard_map(
        shards,
        mesh=mesh,
        in_specs=(P("lev", None, "lat", None), P(), P(), P(("lat", "lev"), None, None)),
        out_specs=P(("lat", "lev"), None, None),
        check_vma=False,
    )
```

```python
import functools

import jax
import jax.numpy as jnp
from jax import lax
from jax.experimental import pallas as pl
from jax.experimental.pallas import tpu as pltpu
from jax.sharding import PartitionSpec as P

LANES = 128
SLAB = 32
CHUNK = 104
HELD = 3
NT = (((1,), (1,)), ((), ()))


def pick_kernel(
    pair_hbm, len_hbm, four_ref, leg_ref, out_ref, held_ref, pair_ref, len_ref, four, column, lows, table, keep, mains, tails, wide, sems
):
    parts, band, waves = four_ref.shape
    half = waves // 2
    slots = leg_ref.shape[0]
    owners = pair_ref.shape[0] * LANES // slots
    place = lax.rem(lax.axis_index("lat"), len_ref.shape[0] * LANES // band)
    turn = lax.rem(place, 4)

    small = [
        pltpu.make_async_copy(pair_hbm, pair_ref, sems.at[parts + slots]),
        pltpu.make_async_copy(len_hbm, len_ref, sems.at[parts + slots + 1]),
    ]
    fetches = [pltpu.make_async_copy(four_ref.at[t], four.at[t], sems.at[t]) for t in range(parts)]
    holds = [
        pltpu.make_async_copy(leg_ref.at[s], held_ref.at[s], sems.at[parts + s]) for s in range(HELD)
    ]
    for copy in small + fetches + holds:
        copy.start()
    for copy in small:
        copy.wait()

    def column_of(row):
        return jnp.transpose(jnp.broadcast_to(row, (LANES, LANES)))

    first = lax.div(place * band, LANES)
    for n in range(2):
        limit = jnp.minimum(waves, lax.shift_right_logical(len_ref[pl.ds(first + n, 1), :], 1))
        column[pl.ds(n * LANES, LANES), :] = column_of(limit)
    for n in range(pair_ref.shape[0]):
        lows[pl.ds(n * LANES, LANES), :] = column_of(pair_ref[pl.ds(n, 1), :])
    lane = lax.broadcasted_iota(jnp.int32, (SLAB, LANES), 1)
    for slab in range(band // SLAB):
        edge = column[pl.ds(pl.multiple_of((turn + slab) * SLAB, SLAB), SLAB), :]
        for tile in range(waves // LANES):
            inside = jnp.where(lane + tile * LANES < edge, 1.0, 0.0).astype(jnp.bfloat16)
            keep[pl.ds(slab * SLAB, SLAB), pl.ds(tile * LANES, LANES)] = inside
    lane = lax.broadcasted_iota(jnp.int32, (owners, LANES), 1)
    for s in range(slots):
        low = lows[pl.ds(s, owners, stride=slots), :]
        rows = pl.ds(s * owners, owners)
        for tile in range(half // LANES):
            wave = lane + tile * LANES
            cols = pl.ds(tile * LANES, LANES)
            table[0, rows, cols] = jnp.where(wave == low, 1.0, 0.0).astype(jnp.bfloat16)
            table[1, rows, cols] = jnp.where(wave == half - 1 - low, 1.0, 0.0).astype(jnp.bfloat16)

    def mask(n):
        for h in range(2):
            t = 2 * n + h
            for slab in range(band // SLAB):
                rows = pl.ds(slab * SLAB, SLAB)
                value = four[t, rows, :] * keep[rows, :]
                if slab < 4:
                    start = h * LANES + lax.rem(slab + turn, 4) * SLAB
                    mains[n][pl.ds(pl.multiple_of(start, SLAB), SLAB), :] = value
                else:
                    tails[pl.ds(t * SLAB, SLAB), :] = value

    def picked(k, rows):
        return lax.dot_general(
            table[k], rows[:, half * k : half * (k + 1)], NT, preferred_element_type=jnp.float32
        )

    def wait(n):
        fetches[2 * n].wait()
        fetches[2 * n + 1].wait()

    def place_main(n):
        rows = mains[n][...]
        for k in range(2):
            value = picked(k, rows)
            for s in range(slots):
                for h in range(2):
                    start = 16 * s + 8 * k + 2 * n + h
                    wide[pl.ds(start, owners, stride=CHUNK), :] = value[
                        s * owners : (s + 1) * owners, h * LANES : (h + 1) * LANES
                    ]

    for n in range(parts // 2):
        wait(n)
        mask(n)
    lane = lax.broadcasted_iota(jnp.int32, (owners, LANES), 1)
    rows = tails[...]
    values = [picked(k, rows) for k in range(2)]
    place_main(0)

    def piece(k, s, h):
        return values[k][s * owners : (s + 1) * owners, h * LANES : (h + 1) * LANES]

    def exchange(x, y, apart):
        low = (lane & (apart * SLAB)) == 0
        back = LANES - apart * SLAB
        return (
            jnp.where(low, x, pltpu.roll(y, apart * SLAB, 1)),
            jnp.where(low, pltpu.roll(x, back, 1), y),
        )

    for h in range(2):
        for k in range(2):
            v = [piece(k, s, h) for s in range(4)]
            v[0], v[2] = exchange(v[0], v[2], 2)
            v[1], v[3] = exchange(v[1], v[3], 2)
            v[0], v[1] = exchange(v[0], v[1], 1)
            v[2], v[3] = exchange(v[2], v[3], 1)
            for part in range(4):
                start = 16 * slots + 8 * k + 4 * h + part
                wide[pl.ds(start, owners, stride=CHUNK), :] = v[part]
        place_main(1 + h)
        lower, upper = piece(0, 4, h), pltpu.roll(piece(1, 4, h), SLAB, 1)
        for part in range(4):
            out = jnp.where((lane & (3 * SLAB)) == part * SLAB, lower, upper)
            if part:
                out = pltpu.roll(out, LANES - part * SLAB, 1)
            start = 16 * slots + 16 + 4 * h + part
            wide[pl.ds(start, owners, stride=CHUNK), :] = out

    place_main(3)
    block = 16 * CHUNK

    def pack(i, carry):
        rows = pl.ds(pl.multiple_of(i * block, block), block)
        out_ref[rows, :] = wide[rows, :].astype(jnp.bfloat16)
        return carry

    lax.fori_loop(0, owners * CHUNK // block, pack, 0)
    for copy in holds:
        copy.wait()


def sum_kernel(pair_ref, got_ref, held_ref, leg_ref, out_ref, rest, both, rows64, out, leg_sem, out_sem):
    slots, count, loops = leg_ref.shape
    waves = 2 * pair_ref.shape[0]
    half = waves // 2
    groups = loops // (5 * LANES)
    peers = got_ref.shape[0] // CHUNK
    levs = peers // (8 * groups)
    south = peers // 2 * CHUNK
    owner = lax.axis_index("lat") * lax.axis_size("lev") + lax.axis_index("lev")

    fetches = [pltpu.make_async_copy(leg_ref.at[s], rest.at[s - HELD], leg_sem.at[s]) for s in range(HELD, slots)]
    for fetch in fetches:
        fetch.start()

    lane = lax.broadcasted_iota(jnp.int32, (16, LANES), 1)

    def pair_of(src, start, size):
        rows = pl.ds(src * CHUNK + start, size)
        north = got_ref[rows, :].astype(jnp.float32)
        rows = pl.ds(src * CHUNK + south + start, size)
        return north, got_ref[rows, :].astype(jnp.float32)

    def combined(pair):
        return pair[0] + pair[1], pair[0] - pair[1]

    def turned(value, by):
        by = (by * SLAB) % LANES
        return pltpu.roll(value, by, 1) if by else value

    def build(s):
        for j in range(levs):
            for g in range(groups):
                mains, tails = [], []
                for b in range(4):
                    src = (4 * g + b) * levs + j
                    mains.append(combined(pair_of(src, 16 * s, 16)))
                    if s < 4:
                        ends = combined(pair_of(src, 16 * slots, 16))
                        tails.append([turned(e, b - s) for e in ends])
                    else:
                        ends = combined(pair_of(src, 16 * slots + 16, 8))
                        tails.append([jnp.concatenate([turned(e, b), turned(e, b - 1)], 0) for e in ends])
                for p in range(2):
                    m = [x[p] for x in mains]
                    e = [x[p] for x in tails]
                    tiles = (
                        m[0],
                        jnp.where(lane < 32, e[0], m[1]),
                        jnp.where(lane < 32, m[1], jnp.where(lane < 64, e[1], m[2])),
                        jnp.where(lane < 64, m[2], jnp.where(lane < 96, e[2], m[3])),
                        jnp.where(lane < 96, m[3], e[3]),
                    )
                    for i, tile in enumerate(tiles):
                        cols = pl.ds((5 * g + i) * LANES, LANES)
                        both[s][p, pl.ds(16 * j, 16), cols] = tile.astype(jnp.bfloat16)

    tiles = half // LANES
    dot = functools.partial(lax.dot_general, dimension_numbers=NT, preferred_element_type=jnp.float32)

    def sums(s):
        if s >= HELD:
            fetches[s - HELD].wait()
        leg = held_ref.at[s] if s < HELD else rest.at[s - HELD]
        sym = dot(both[s][0], leg[pl.ds(0, half + 16), :])
        anti = dot(both[s][1], leg[pl.ds(half, count - half), :])
        return sym, anti

    def finish(s, sym, anti):
        low = pair_ref[owner * slots + s]
        sym_limit = lax.shift_right_logical(waves - low + 1, 1)
        anti_limit = lax.shift_right_logical(waves - low, 1) + half + 1
        for j in range(levs):
            first = slice(16 * j, 16 * j + 8)
            second = slice(16 * j + 8, 16 * j + 16)
            for i in range(tiles):
                at = lax.broadcasted_iota(jnp.int32, (8, LANES), 1) + i * LANES
                cols = slice(i * LANES, (i + 1) * LANES)
                rows64[s][i, pl.ds(8 * j, 8), :] = jnp.where(at < sym_limit, sym[first, cols], sym[second, cols])
            for i in range(tiles + 1):
                width = min(LANES, count - half - i * LANES)
                at = lax.broadcasted_iota(jnp.int32, (8, width), 1) + half + i * LANES
                cols = slice(i * LANES, i * LANES + width)
                value = jnp.where(at < anti_limit, anti[first, cols], anti[second, cols])
                if i == 0:
                    middle = slice(half, half + 1)
                    mid = jnp.where(half < sym_limit, sym[first, middle], sym[second, middle])
                    value = jnp.where(at == half, mid, value)
                rows64[s][tiles + i, pl.ds(8 * j, 8), :width] = value
        for i in range(2 * tiles + 1):
            width = min(LANES, count - i * LANES)
            for c in range(2):
                for v in range(levs // 2):
                    value = rows64[s][i, pl.ds(16 * v + c, 8, stride=2), :]
                    out[s][pl.ds(4 * levs * c + 8 * v, 8), pl.ds(i * LANES, width)] = value[:, :width]

    copies = [pltpu.make_async_copy(out[s], out_ref.at[s], out_sem.at[s]) for s in range(slots)]
    build(0)
    for s in range(slots):
        total = sums(s)
        if s + 1 < slots:
            build(s + 1)
        finish(s, *total)
        copies[s].start()
    for copy in copies:
        copy.wait()


def in_hbm(value):
    return pltpu.with_memory_space_constraint(value, pltpu.HBM)


def pick(fourier, loop_len, pair_m, legendre):
    levels, parts, band, waves = fourier.shape
    slots, count, loops = legendre.shape
    owners = pair_m.shape[0] // slots
    half = waves // 2
    hbm = pl.BlockSpec(memory_space=pltpu.HBM)
    vmem = pl.BlockSpec(memory_space=pltpu.VMEM)
    return pl.pallas_call(
        pick_kernel,
        out_shape=(
            jax.ShapeDtypeStruct((owners * CHUNK, LANES), jnp.bfloat16),
            pltpu.VMEM((HELD, count, loops), legendre.dtype),
        ),
        in_specs=[hbm] * 4,
        out_specs=(vmem, vmem),
        scratch_shapes=[
            pltpu.VMEM((owners * slots // LANES, LANES), jnp.int32),
            pltpu.VMEM((loops // LANES, LANES), jnp.int32),
            pltpu.VMEM((levels * parts, band, waves), jnp.bfloat16),
            pltpu.VMEM((2 * LANES, LANES), jnp.int32),
            pltpu.VMEM((owners * slots, LANES), jnp.int32),
            pltpu.VMEM((2, owners * slots, half), jnp.bfloat16),
            pltpu.VMEM((band, waves), jnp.bfloat16),
            [pltpu.VMEM((2 * LANES, waves), jnp.bfloat16)] * (levels * parts // 2),
            pltpu.VMEM((levels * parts * SLAB, waves), jnp.bfloat16),
            pltpu.VMEM((owners * CHUNK, LANES), jnp.float32),
            pltpu.SemaphoreType.DMA((levels * parts + slots + 2,)),
        ],
        compiler_params=pltpu.CompilerParams(vmem_limit_bytes=32 * 2**20),
        name="pick",
    )(
        in_hbm(pair_m.reshape(-1, LANES)),
        in_hbm(loop_len.reshape(-1, LANES)),
        in_hbm(fourier.reshape(levels * parts, band, waves)),
        in_hbm(legendre),
    )


def transform(pair_m, arrived, held, legendre):
    slots, count, loops = legendre.shape
    vmem = pl.BlockSpec(memory_space=pltpu.VMEM)
    out = pl.pallas_call(
        sum_kernel,
        out_shape=jax.ShapeDtypeStruct((slots, 64, count), jnp.float32),
        in_specs=[pl.BlockSpec(memory_space=pltpu.SMEM), vmem, vmem, pl.BlockSpec(memory_space=pltpu.HBM)],
        out_specs=pl.BlockSpec(memory_space=pl.ANY),
        scratch_shapes=[
            pltpu.VMEM((slots - HELD, count, loops), jnp.bfloat16),
            [pltpu.VMEM((2, 128, loops), jnp.bfloat16)] * slots,
            [pltpu.VMEM((count // LANES + 1, 64, LANES), jnp.float32)] * slots,
            [pltpu.VMEM((64, count), jnp.float32)] * slots,
            pltpu.SemaphoreType.DMA((slots,)),
            pltpu.SemaphoreType.DMA((slots,)),
        ],
        compiler_params=pltpu.CompilerParams(vmem_limit_bytes=28 * 2**20),
        name="transform",
    )(pair_m, arrived, held, in_hbm(legendre))
    return jnp.transpose(out, (0, 2, 1))


def shards(fourier, loop_len, pair_m, legendre):
    outgoing, held = pick(fourier, loop_len, pair_m, legendre)
    chunks = outgoing.reshape(-1, CHUNK, LANES)
    arrived = lax.all_to_all(chunks, ("lat", "lev"), split_axis=0, concat_axis=0, tiled=True)
    return transform(pair_m, arrived.reshape(-1, LANES), held, legendre)


def solution(mesh):
    return jax.shard_map(
        shards,
        mesh=mesh,
        in_specs=(P("lev", None, "lat", None), P(), P(), P(("lat", "lev"), None, None)),
        out_specs=P(("lat", "lev"), None, None),
        check_vma=False,
    )
```

```python
import functools

import jax
import jax.numpy as jnp
from jax import lax
from jax.experimental import pallas as pl
from jax.experimental.pallas import tpu as pltpu
from jax.sharding import PartitionSpec as P

LANES = 128
SLAB = 32
CHUNK = 104
HELD = 3
NT = (((1,), (1,)), ((), ()))


def pick_kernel(
    pair_hbm, len_hbm, four_ref, leg_ref, out_ref, held_ref, pair_ref, len_ref, four, column, lows, table, keep, mains, tails, wide, sems
):
    parts, band, waves = four_ref.shape
    half = waves // 2
    slots = leg_ref.shape[0]
    owners = pair_ref.shape[0] * LANES // slots
    place = lax.rem(lax.axis_index("lat"), len_ref.shape[0] * LANES // band)
    turn = lax.rem(place, 4)

    small = [
        pltpu.make_async_copy(pair_hbm, pair_ref, sems.at[parts + slots]),
        pltpu.make_async_copy(len_hbm, len_ref, sems.at[parts + slots + 1]),
    ]
    fetches = [pltpu.make_async_copy(four_ref.at[t], four.at[t], sems.at[t]) for t in range(parts)]
    holds = [
        pltpu.make_async_copy(leg_ref.at[s], held_ref.at[s], sems.at[parts + s]) for s in range(HELD)
    ]
    for copy in small + fetches + holds:
        copy.start()
    for copy in small:
        copy.wait()

    def column_of(row):
        return jnp.transpose(jnp.broadcast_to(row, (LANES, LANES)))

    first = lax.div(place * band, LANES)
    for n in range(2):
        limit = jnp.minimum(waves, lax.shift_right_logical(len_ref[pl.ds(first + n, 1), :], 1))
        column[pl.ds(n * LANES, LANES), :] = column_of(limit)
    for n in range(pair_ref.shape[0]):
        lows[pl.ds(n * LANES, LANES), :] = column_of(pair_ref[pl.ds(n, 1), :])
    lane = lax.broadcasted_iota(jnp.int32, (SLAB, LANES), 1)
    for slab in range(band // SLAB):
        edge = column[pl.ds(pl.multiple_of((turn + slab) * SLAB, SLAB), SLAB), :]
        for tile in range(waves // LANES):
            inside = jnp.where(lane + tile * LANES < edge, 1.0, 0.0).astype(jnp.bfloat16)
            keep[pl.ds(slab * SLAB, SLAB), pl.ds(tile * LANES, LANES)] = inside
    lane = lax.broadcasted_iota(jnp.int32, (owners, LANES), 1)
    for s in range(slots):
        low = lows[pl.ds(s, owners, stride=slots), :]
        rows = pl.ds(s * owners, owners)
        for tile in range(half // LANES):
            wave = lane + tile * LANES
            cols = pl.ds(tile * LANES, LANES)
            table[0, rows, cols] = jnp.where(wave == low, 1.0, 0.0).astype(jnp.bfloat16)
            table[1, rows, cols] = jnp.where(wave == half - 1 - low, 1.0, 0.0).astype(jnp.bfloat16)

    def mask(n):
        for h in range(2):
            t = 2 * n + h
            for slab in range(band // SLAB):
                rows = pl.ds(slab * SLAB, SLAB)
                value = four[t, rows, :] * keep[rows, :]
                if slab < 4:
                    start = h * LANES + lax.rem(slab + turn, 4) * SLAB
                    mains[n][pl.ds(pl.multiple_of(start, SLAB), SLAB), :] = value
                else:
                    tails[pl.ds(t * SLAB, SLAB), :] = value

    def picked(k, rows):
        return lax.dot_general(
            table[k], rows[:, half * k : half * (k + 1)], NT, preferred_element_type=jnp.float32
        )

    def wait(n):
        fetches[2 * n].wait()
        fetches[2 * n + 1].wait()

    def place_main(n):
        rows = mains[n][...]
        for k in range(2):
            value = picked(k, rows)
            for s in range(slots):
                for h in range(2):
                    start = 16 * s + 8 * k + 2 * n + h
                    wide[pl.ds(start, owners, stride=CHUNK), :] = value[
                        s * owners : (s + 1) * owners, h * LANES : (h + 1) * LANES
                    ]

    for n in range(parts // 2):
        wait(n)
        mask(n)
    lane = lax.broadcasted_iota(jnp.int32, (owners, LANES), 1)
    rows = tails[...]
    values = [picked(k, rows) for k in range(2)]
    place_main(0)

    def piece(k, s, h):
        return values[k][s * owners : (s + 1) * owners, h * LANES : (h + 1) * LANES]

    def exchange(x, y, apart):
        low = (lane & (apart * SLAB)) == 0
        back = LANES - apart * SLAB
        return (
            jnp.where(low, x, pltpu.roll(y, apart * SLAB, 1)),
            jnp.where(low, pltpu.roll(x, back, 1), y),
        )

    for h in range(2):
        for k in range(2):
            v = [piece(k, s, h) for s in range(4)]
            v[0], v[2] = exchange(v[0], v[2], 2)
            v[1], v[3] = exchange(v[1], v[3], 2)
            v[0], v[1] = exchange(v[0], v[1], 1)
            v[2], v[3] = exchange(v[2], v[3], 1)
            for part in range(4):
                start = 16 * slots + 8 * k + 4 * h + part
                wide[pl.ds(start, owners, stride=CHUNK), :] = v[part]
        place_main(1 + h)
        lower, upper = piece(0, 4, h), pltpu.roll(piece(1, 4, h), SLAB, 1)
        for part in range(4):
            out = jnp.where((lane & (3 * SLAB)) == part * SLAB, lower, upper)
            if part:
                out = pltpu.roll(out, LANES - part * SLAB, 1)
            start = 16 * slots + 16 + 4 * h + part
            wide[pl.ds(start, owners, stride=CHUNK), :] = out

    place_main(3)
    block = 16 * CHUNK

    def pack(i, carry):
        rows = pl.ds(pl.multiple_of(i * block, block), block)
        out_ref[rows, :] = wide[rows, :].astype(jnp.bfloat16)
        return carry

    lax.fori_loop(0, owners * CHUNK // block, pack, 0, unroll=True)
    for copy in holds:
        copy.wait()


def sum_kernel(pair_ref, got_ref, held_ref, leg_ref, out_ref, rest, both, rows64, out, leg_sem, out_sem):
    slots, count, loops = leg_ref.shape
    waves = 2 * pair_ref.shape[0]
    half = waves // 2
    groups = loops // (5 * LANES)
    peers = got_ref.shape[0] // CHUNK
    levs = peers // (8 * groups)
    south = peers // 2 * CHUNK
    owner = lax.axis_index("lat") * lax.axis_size("lev") + lax.axis_index("lev")

    fetches = [pltpu.make_async_copy(leg_ref.at[s], rest.at[s - HELD], leg_sem.at[s]) for s in range(HELD, slots)]
    for fetch in fetches:
        fetch.start()

    lane = lax.broadcasted_iota(jnp.int32, (16, LANES), 1)

    def pair_of(src, start, size):
        rows = pl.ds(src * CHUNK + start, size)
        north = got_ref[rows, :].astype(jnp.float32)
        rows = pl.ds(src * CHUNK + south + start, size)
        return north, got_ref[rows, :].astype(jnp.float32)

    def combined(pair):
        return pair[0] + pair[1], pair[0] - pair[1]

    def turned(value, by):
        by = (by * SLAB) % LANES
        return pltpu.roll(value, by, 1) if by else value

    def build(s):
        for j in range(levs):
            for g in range(groups):
                mains, tails = [], []
                for b in range(4):
                    src = (4 * g + b) * levs + j
                    mains.append(combined(pair_of(src, 16 * s, 16)))
                    if s < 4:
                        ends = combined(pair_of(src, 16 * slots, 16))
                        tails.append([turned(e, b - s) for e in ends])
                    else:
                        ends = combined(pair_of(src, 16 * slots + 16, 8))
                        tails.append([jnp.concatenate([turned(e, b), turned(e, b - 1)], 0) for e in ends])
                for p in range(2):
                    m = [x[p] for x in mains]
                    e = [x[p] for x in tails]
                    tiles = (
                        m[0],
                        jnp.where(lane < 32, e[0], m[1]),
                        jnp.where(lane < 32, m[1], jnp.where(lane < 64, e[1], m[2])),
                        jnp.where(lane < 64, m[2], jnp.where(lane < 96, e[2], m[3])),
                        jnp.where(lane < 96, m[3], e[3]),
                    )
                    for i, tile in enumerate(tiles):
                        cols = pl.ds((5 * g + i) * LANES, LANES)
                        both[s][p, pl.ds(16 * j, 16), cols] = tile.astype(jnp.bfloat16)

    tiles = half // LANES
    dot = functools.partial(lax.dot_general, dimension_numbers=NT, preferred_element_type=jnp.float32)

    def sums(s):
        if s >= HELD:
            fetches[s - HELD].wait()
        leg = held_ref.at[s] if s < HELD else rest.at[s - HELD]
        sym = dot(both[s][0], leg[pl.ds(0, half + 16), :])
        anti = dot(both[s][1], leg[pl.ds(half, count - half), :])
        return sym, anti

    def finish(s, sym, anti):
        low = pair_ref[owner * slots + s]
        sym_limit = lax.shift_right_logical(waves - low + 1, 1)
        anti_limit = lax.shift_right_logical(waves - low, 1) + half + 1
        for j in range(levs):
            first = slice(16 * j, 16 * j + 8)
            second = slice(16 * j + 8, 16 * j + 16)
            for i in range(tiles):
                at = lax.broadcasted_iota(jnp.int32, (8, LANES), 1) + i * LANES
                cols = slice(i * LANES, (i + 1) * LANES)
                rows64[s][i, pl.ds(8 * j, 8), :] = jnp.where(at < sym_limit, sym[first, cols], sym[second, cols])
            for i in range(tiles + 1):
                width = min(LANES, count - half - i * LANES)
                at = lax.broadcasted_iota(jnp.int32, (8, width), 1) + half + i * LANES
                cols = slice(i * LANES, i * LANES + width)
                value = jnp.where(at < anti_limit, anti[first, cols], anti[second, cols])
                if i == 0:
                    middle = slice(half, half + 1)
                    mid = jnp.where(half < sym_limit, sym[first, middle], sym[second, middle])
                    value = jnp.where(at == half, mid, value)
                rows64[s][tiles + i, pl.ds(8 * j, 8), :width] = value
        for i in range(2 * tiles + 1):
            width = min(LANES, count - i * LANES)
            for c in range(2):
                for v in range(levs // 2):
                    value = rows64[s][i, pl.ds(16 * v + c, 8, stride=2), :]
                    out[s][pl.ds(4 * levs * c + 8 * v, 8), pl.ds(i * LANES, width)] = value[:, :width]

    copies = [pltpu.make_async_copy(out[s], out_ref.at[s], out_sem.at[s]) for s in range(slots)]
    build(0)
    for s in range(slots):
        total = sums(s)
        if s + 1 < slots:
            build(s + 1)
        finish(s, *total)
        copies[s].start()
    for copy in copies:
        copy.wait()


def in_hbm(value):
    return pltpu.with_memory_space_constraint(value, pltpu.HBM)


def pick(fourier, loop_len, pair_m, legendre):
    levels, parts, band, waves = fourier.shape
    slots, count, loops = legendre.shape
    owners = pair_m.shape[0] // slots
    half = waves // 2
    hbm = pl.BlockSpec(memory_space=pltpu.HBM)
    vmem = pl.BlockSpec(memory_space=pltpu.VMEM)
    return pl.pallas_call(
        pick_kernel,
        out_shape=(
            jax.ShapeDtypeStruct((owners * CHUNK, LANES), jnp.bfloat16),
            pltpu.VMEM((HELD, count, loops), legendre.dtype),
        ),
        in_specs=[hbm] * 4,
        out_specs=(vmem, vmem),
        scratch_shapes=[
            pltpu.VMEM((owners * slots // LANES, LANES), jnp.int32),
            pltpu.VMEM((loops // LANES, LANES), jnp.int32),
            pltpu.VMEM((levels * parts, band, waves), jnp.bfloat16),
            pltpu.VMEM((2 * LANES, LANES), jnp.int32),
            pltpu.VMEM((owners * slots, LANES), jnp.int32),
            pltpu.VMEM((2, owners * slots, half), jnp.bfloat16),
            pltpu.VMEM((band, waves), jnp.bfloat16),
            [pltpu.VMEM((2 * LANES, waves), jnp.bfloat16)] * (levels * parts // 2),
            pltpu.VMEM((levels * parts * SLAB, waves), jnp.bfloat16),
            pltpu.VMEM((owners * CHUNK, LANES), jnp.float32),
            pltpu.SemaphoreType.DMA((levels * parts + slots + 2,)),
        ],
        compiler_params=pltpu.CompilerParams(vmem_limit_bytes=32 * 2**20),
        name="pick",
    )(
        in_hbm(pair_m.reshape(-1, LANES)),
        in_hbm(loop_len.reshape(-1, LANES)),
        in_hbm(fourier.reshape(levels * parts, band, waves)),
        in_hbm(legendre),
    )


def transform(pair_m, arrived, held, legendre):
    slots, count, loops = legendre.shape
    vmem = pl.BlockSpec(memory_space=pltpu.VMEM)
    out = pl.pallas_call(
        sum_kernel,
        out_shape=jax.ShapeDtypeStruct((slots, 64, count), jnp.float32),
        in_specs=[pl.BlockSpec(memory_space=pltpu.SMEM), vmem, vmem, pl.BlockSpec(memory_space=pltpu.HBM)],
        out_specs=pl.BlockSpec(memory_space=pl.ANY),
        scratch_shapes=[
            pltpu.VMEM((slots - HELD, count, loops), jnp.bfloat16),
            [pltpu.VMEM((2, 128, loops), jnp.bfloat16)] * slots,
            [pltpu.VMEM((count // LANES + 1, 64, LANES), jnp.float32)] * slots,
            [pltpu.VMEM((64, count), jnp.float32)] * slots,
            pltpu.SemaphoreType.DMA((slots,)),
            pltpu.SemaphoreType.DMA((slots,)),
        ],
        compiler_params=pltpu.CompilerParams(vmem_limit_bytes=28 * 2**20),
        name="transform",
    )(pair_m, arrived, held, in_hbm(legendre))
    return jnp.transpose(out, (0, 2, 1))


def shards(fourier, loop_len, pair_m, legendre):
    outgoing, held = pick(fourier, loop_len, pair_m, legendre)
    chunks = outgoing.reshape(-1, CHUNK, LANES)
    arrived = lax.all_to_all(chunks, ("lat", "lev"), split_axis=0, concat_axis=0, tiled=True)
    return transform(pair_m, arrived.reshape(-1, LANES), held, legendre)


def solution(mesh):
    return jax.shard_map(
        shards,
        mesh=mesh,
        in_specs=(P("lev", None, "lat", None), P(), P(), P(("lat", "lev"), None, None)),
        out_specs=P(("lat", "lev"), None, None),
        check_vma=False,
    )
```
